512 devices in a mesh: row: 32 (over x, y_lo, core), col: 16 (over y_hi, z).
Axes of the slice: x: 4, y: 8 (y_hi: 2, y_lo: 4; y = y_hi * 4 + y_lo), z: 8, core: 2. Of those that a mesh axis runs over, the one named last changes fastest.
Arguments:
- covariance: bfloat16 [24576, 24576], P('row', 'col'), as said below
Outputs:
- trailing: bfloat16 [24576, 24576], P('row', 'col')
Inputs may be any that keep to these rules, and one draw needn't show every extreme that they name: covariance is symmetric, and its leading 3 * 256 rows and columns form a positive definite block.
All inputs are finite; a program needn't handle non-finite values.
Results may differ from the reference program's by a relative error of at most 0.0058.
Values may be sent and summed in bfloat16 or wider, within the bound.
No kernel may reach another device: no remote copies, remote signals or barrier semaphores. Data moves between devices by JAX's collectives and lax.ppermute only.
A program may use at most 64 MiB of HBM per device.

```python
import math
import jax
import jax.numpy as jnp
from jax import lax

M = 24576
NB = 256
ITERS = 3


def draw_covariance(key, part):
    key = jax.random.fold_in(key, 7)
    key_noise, key_diag = jax.random.split(key, 2)
    leading = ITERS * NB
    noise_field = jax.random.uniform(key_noise, (M, M), jnp.float32, -1.0, 1.0) * math.sqrt(3.0)
    row_scale = jnp.ones((M,), jnp.float32)
    symmetric = (noise_field + noise_field.T) * math.sqrt(0.5)
    index_vec = jnp.arange(M)
    row_scale = jnp.where(index_vec >= leading, row_scale, 1.0)
    diag_vals = jax.random.uniform(key_diag, (M,), jnp.float32, leading / 4.0, leading / 2.0)
    in_lead = (index_vec < leading)[:, None] & (index_vec < leading)[None, :]
    on_diag = index_vec[:, None] == index_vec[None, :]
    lead_part = jnp.where(on_diag, diag_vals[:, None], 0.09 * math.sqrt(leading) * symmetric)
    outer_part = symmetric * row_scale[:, None] * row_scale[None, :]
    entries = jnp.where(in_lead, lead_part, outer_part)
    return entries.astype(jnp.bfloat16)


def setup_inputs(seed: int = 0) -> dict:
    splits = jax.random.split(jax.random.key(seed), 2)
    covariance = draw_covariance(jax.random.fold_in(splits[1], 71), 0)
    return dict(covariance=covariance)


def reference(covariance):
    current = covariance
    row_index = jnp.arange(M)
    for iteration in range(ITERS):
        first_col = iteration * NB
        panel_cols = current[:, first_col:first_col + NB].astype(jnp.float32)
        diag_block = current[first_col:first_col + NB, first_col:first_col + NB].astype(jnp.float32)
        factor = jnp.linalg.cholesky(diag_block)
        inverse = jax.scipy.linalg.solve_triangular(factor, jnp.eye(NB, dtype=jnp.float32), lower=True)
        solved = jnp.dot(panel_cols, inverse.T, precision=lax.Precision.HIGHEST)
        lower_rows = jnp.where((row_index >= first_col)[:, None], solved, jnp.float32(0.0)).astype(jnp.bfloat16)
        row_blocks = current.reshape(M // NB, NB, M)
        factor_blocks = lower_rows.reshape(M // NB, NB, NB)

        def update(operands):
            block_rows, block_factor = operands
            product = lax.dot_general(block_factor.astype(jnp.float32), lower_rows.astype(jnp.float32), (((1,), (1,)), ((), ())), preferred_element_type=jnp.float32)
            return (block_rows.astype(jnp.float32) - product).astype(jnp.bfloat16)
        current = lax.map(update, (row_blocks, factor_blocks)).reshape(M, M)
    done = ITERS * NB
    trailing_mask = (row_index >= done)[:, None] & (row_index >= done)[None, :]
    return jnp.where(trailing_mask, current, jnp.zeros_like(current)).astype(jnp.bfloat16)
```

```python
import jax
import jax.numpy as jnp
from jax import lax
from jax.experimental import pallas as pl
from jax.experimental.pallas import tpu as pltpu
from jax.sharding import PartitionSpec as P

N = 768
B = 128
STEPS = N // B
HI = lax.Precision.HIGHEST


def mm(a, b):
    return jnp.dot(a, b, precision=HI, preferred_element_type=jnp.float32)


def mm_t(a, b):
    return lax.dot_general(
        a, b, (((0,), (0,)), ((), ())), precision=HI, preferred_element_type=jnp.float32
    )


def invert_factor(block):
    groups = B // 8
    lane = lax.broadcasted_iota(jnp.int32, (8, B), 1)
    sub = lax.broadcasted_iota(jnp.int32, (8, B), 0)
    left = [block[8 * g : 8 * g + 8] for g in range(groups)]
    right = [jnp.where(lane == sub + 8 * g, 1.0, 0.0).astype(jnp.float32) for g in range(groups)]
    done = []

    def over_rows(x, i):
        return jnp.broadcast_to(x[i : i + 1], (8, B))

    def over_lanes(x, i):
        return jnp.broadcast_to(x[:, i : i + 1], (8, B))

    for g in range(groups):
        first = 8 * g
        last = g == groups - 1
        row_l, row_r = left[g], right[g]
        own = [over_lanes(row_l, first + i) for i in range(8)]
        if not last:
            nxt_l, nxt_r = left[g + 1], right[g + 1]
            nxt = [over_lanes(nxt_l, first + i) for i in range(8)]
        pivot = jnp.ones((8, B), jnp.float32)
        for i in range(8):
            d = over_rows(own[i], i)
            r = 1.0 / d
            pivot = jnp.where(sub == i, d, pivot)
            m = jnp.where(sub > i, own[i] * r, 0.0)
            rows = [over_rows(own[t], i) for t in range(i + 1, 8)]
            for t in range(i + 1, 8):
                own[t] = own[t] - m * rows[t - i - 1]
            rl, rr = over_rows(row_l, i), over_rows(row_r, i)
            row_l = row_l - m * rl
            row_r = row_r - m * rr
            if not last:
                n = nxt[i] * r
                for t in range(i + 1, 8):
                    nxt[t] = nxt[t] - n * rows[t - i - 1]
                nxt_l = nxt_l - n * rl
                nxt_r = nxt_r - n * rr
        scale = lax.rsqrt(pivot)
        done.append(row_r * scale)
        if not last:
            left[g + 1], right[g + 1] = nxt_l, nxt_r
        if g + 2 < groups:
            ul = row_l * scale
            cut = jnp.where(lane >= first + 16, ul, 0.0)
            both = mm_t(cut, jnp.concatenate([ul, row_r * scale], axis=1))
            for q in range(g + 2, groups):
                left[q] = left[q] - both[8 * q : 8 * q + 8, :B]
                right[q] = right[q] - both[8 * q : 8 * q + 8, B:]
    return jnp.concatenate(done, axis=0)


def chol_kernel(a_ref, hi_ref, lo_ref, s_ref, w_ref):
    s_ref[...] = a_ref[...].astype(jnp.float32)
    w_ref[...] = jnp.zeros_like(w_ref)
    for k in range(STEPS):
        lo, hi = k * B, (k + 1) * B
        inv = invert_factor(s_ref[lo:hi, lo:hi])
        w_ref[lo:hi, lo:hi] = inv
        if k:
            w_ref[lo:hi, :lo] = mm(inv, w_ref[lo:hi, :lo])
        if hi < N:
            u = mm(inv, s_ref[lo:hi, hi:])
            for q in range(k + 1, STEPS):
                a, b = q * B, (q + 1) * B
                uq = u[:, a - hi : b - hi]
                s_ref[a:b, a:] = s_ref[a:b, a:] - mm_t(uq, u[:, a - hi :])
                w_ref[a:b, :hi] = w_ref[a:b, :hi] - mm_t(uq, w_ref[lo:hi, :hi])
    w = w_ref[...]
    high = w.astype(jnp.bfloat16)
    hi_ref[...] = high
    lo_ref[...] = (w - high.astype(jnp.float32)).astype(jnp.bfloat16)


def chol(a):
    vm = pl.BlockSpec(memory_space=pltpu.VMEM)
    return pl.pallas_call(
        chol_kernel,
        out_shape=[jax.ShapeDtypeStruct((N, N), jnp.bfloat16)] * 2,
        in_specs=[vm],
        out_specs=[vm, vm],
        scratch_shapes=[pltpu.VMEM((N, N), jnp.float32), pltpu.VMEM((N, N), jnp.float32)],
        compiler_params=pltpu.CompilerParams(vmem_limit_bytes=16 << 20),
        cost_estimate=pl.CostEstimate(flops=48_000_000_000, bytes_accessed=4_000_000, transcendentals=0),
        name="factor",
    )(a)


TILE = 256
PANEL = 256


def update_kernel(where_ref, cov_ref, rows_ref, mine_ref, other_ref, hi_ref, lo_ref, out_ref, left_ref):
    row, col, core = where_ref[0], where_ref[1], where_ref[2]
    step = pl.program_id(0)

    @pl.when(step == 0)
    def _():
        for k in range(N // PANEL):
            lo, hi = k * PANEL, (k + 1) * PANEL
            part = jnp.zeros((rows_ref.shape[0], PANEL), jnp.float32)
            for w_ref in (hi_ref, lo_ref):
                part += lax.dot_general(
                    rows_ref[:, :hi],
                    w_ref[lo:hi, :hi],
                    (((1,), (1,)), ((), ())),
                    preferred_element_type=jnp.float32,
                )
            left_ref[:, lo:hi] = part.astype(jnp.bfloat16)

    half = lax.div(step, N // TILE)
    at = pl.multiple_of(lax.rem(step, N // TILE) * TILE, TILE)
    panel = jnp.where(half == core, mine_ref[:, pl.ds(at, TILE)], other_ref[:, pl.ds(at, TILE)])
    parts = []
    for k in range(N // PANEL):
        lo, hi = k * PANEL, (k + 1) * PANEL
        part = jnp.dot(hi_ref[lo:hi, :hi], panel[:hi], preferred_element_type=jnp.float32)
        part += jnp.dot(lo_ref[lo:hi, :hi], panel[:hi], preferred_element_type=jnp.float32)
        parts.append(part.astype(jnp.bfloat16))
    right = jnp.concatenate(parts, axis=0)
    product = jnp.dot(left_ref[...], right, preferred_element_type=jnp.float32)
    value = (cov_ref[...].astype(jnp.float32) - product).astype(jnp.bfloat16)
    keep = jnp.logical_and(row > 0, jnp.logical_or(col > 0, half > 0))
    out_ref[...] = jnp.where(keep, value, jnp.zeros_like(value))


def update(place, cov, rows, mine, other, hi, lo):
    n_rows, n_cols = cov.shape
    vm = pl.BlockSpec(memory_space=pltpu.VMEM)
    tile = pl.BlockSpec((n_rows, TILE), lambda j: (0, j))
    return pl.pallas_call(
        update_kernel,
        out_shape=jax.ShapeDtypeStruct(cov.shape, jnp.bfloat16),
        grid=(n_cols // TILE,),
        in_specs=[pl.BlockSpec(memory_space=pltpu.SMEM), tile, vm, vm, vm, vm, vm],
        out_specs=tile,
        scratch_shapes=[pltpu.VMEM((n_rows, N), jnp.bfloat16)],
        compiler_params=pltpu.CompilerParams(vmem_limit_bytes=24 << 20),
        name="update",
    )(place, cov, rows, mine, other, hi, lo)


CHIPS = 16
PIECE = N // CHIPS
SAME_CORE = [[2 * chip + core for chip in range(CHIPS)] for core in range(2)]


def spread_rows(piece):
    sent = [lax.ppermute(piece, "row", [(0, 8 * x)]) for x in (2, 1, 3)]
    piece = sent[0] + sent[1] + sent[2] + jnp.where(lax.axis_index("row") == 0, piece, 0)
    pairs = lambda y: [(8 * x, 8 * x + 2 * y) for x in range(4)]
    sent = [lax.ppermute(piece, "row", pairs(y)) for y in (3, 2, 1)]
    piece = sent[0] + sent[1] + sent[2] + piece
    return piece + lax.ppermute(piece, "row", [(2 * chip, 2 * chip + 1) for chip in range(CHIPS)])


def scatter(x, axis, groups=None):
    return lax.all_to_all(x, axis, 0, 0, axis_index_groups=groups, tiled=True)[:PIECE]


def gather(piece, axis, groups=None):
    same = jnp.broadcast_to(piece[None], (CHIPS, *piece.shape)).reshape(-1, piece.shape[1])
    return lax.all_to_all(same, axis, 0, 0, axis_index_groups=groups, tiled=True)


def per_device(covariance):
    row = lax.axis_index("row")
    col = lax.axis_index("col")
    core = lax.rem(row, 2)
    first = covariance[:, :N]
    passed = lax.ppermute(covariance[:, N:], "row", [(0, 1)])
    rows_piece = scatter(first, "col")
    cols_piece = scatter(jnp.where(row == 1, passed, first), "row", SAME_CORE)
    leading = gather(spread_rows(rows_piece), "col")
    hi, lo = chol(leading)
    rows = gather(rows_piece, "col")
    mine = gather(cols_piece, "row", SAME_CORE)
    other = lax.ppermute(mine, "row", [(r, r ^ 1) for r in range(2 * CHIPS)])
    place = jnp.stack([row, col, core]).astype(jnp.int32)
    return update(place, covariance, rows, mine, other, hi, lo)


def solution(mesh):
    return jax.shard_map(
        per_device,
        mesh=mesh,
        in_specs=(P("row", "col"),),
        out_specs=P("row", "col"),
        check_vma=False,
    )
```

```python
import jax
import jax.numpy as jnp
from jax import lax
from jax.experimental import pallas as pl
from jax.experimental.pallas import tpu as pltpu
from jax.sharding import PartitionSpec as P

N = 768
B = 128
STEPS = N // B
HI = lax.Precision.HIGHEST


def mm(a, b):
    return jnp.dot(a, b, precision=HI, preferred_element_type=jnp.float32)


def mm_t(a, b):
    return lax.dot_general(
        a, b, (((0,), (0,)), ((), ())), precision=HI, preferred_element_type=jnp.float32
    )


def invert_factor(block):
    groups = B // 8
    lane = lax.broadcasted_iota(jnp.int32, (8, B), 1)
    sub = lax.broadcasted_iota(jnp.int32, (8, B), 0)
    left = [block[8 * g : 8 * g + 8] for g in range(groups)]
    right = [jnp.where(lane == sub + 8 * g, 1.0, 0.0).astype(jnp.float32) for g in range(groups)]
    done = []

    def over_rows(x, i):
        return jnp.broadcast_to(x[i : i + 1], (8, B))

    def over_lanes(x, i):
        return jnp.broadcast_to(x[:, i : i + 1], (8, B))

    for g in range(groups):
        first = 8 * g
        last = g == groups - 1
        row_l, row_r = left[g], right[g]
        own = [over_lanes(row_l, first + i) for i in range(8)]
        if not last:
            nxt_l, nxt_r = left[g + 1], right[g + 1]
            nxt = [over_lanes(nxt_l, first + i) for i in range(8)]
        pivot = jnp.ones((8, B), jnp.float32)
        for i in range(8):
            d = over_rows(own[i], i)
            r = 1.0 / d
            pivot = jnp.where(sub == i, d, pivot)
            m = jnp.where(sub > i, own[i] * r, 0.0)
            rows = [over_rows(own[t], i) for t in range(i + 1, 8)]
            for t in range(i + 1, 8):
                own[t] = own[t] - m * rows[t - i - 1]
            rl, rr = over_rows(row_l, i), over_rows(row_r, i)
            row_l = row_l - m * rl
            row_r = row_r - m * rr
            if not last:
                n = nxt[i] * r
                for t in range(i + 1, 8):
                    nxt[t] = nxt[t] - n * rows[t - i - 1]
                nxt_l = nxt_l - n * rl
                nxt_r = nxt_r - n * rr
        scale = lax.rsqrt(pivot)
        done.append(row_r * scale)
        if not last:
            left[g + 1], right[g + 1] = nxt_l, nxt_r
        if g + 2 < groups:
            ul = row_l * scale
            cut = jnp.where(lane >= first + 16, ul, 0.0)
            both = mm_t(cut, jnp.concatenate([ul, row_r * scale], axis=1))
            for q in range(g + 2, groups):
                left[q] = left[q] - both[8 * q : 8 * q + 8, :B]
                right[q] = right[q] - both[8 * q : 8 * q + 8, B:]
    return jnp.concatenate(done, axis=0)


BANDS = STEPS // 2
FOLD = (STEPS + 1) * B
SPLIT = 3
CUT = SPLIT * B


def fold(a):
    bands = []
    for k in range(BANDS):
        j = STEPS - 1 - k
        bands.append(jnp.concatenate([a[k * B : (k + 1) * B, k * B :], a[j * B : (j + 1) * B, j * B :]], axis=1))
    return jnp.concatenate(bands, axis=0)


def eliminate(k, s_ref, w_ref, base):
    lo, hi = k * B, (k + 1) * B
    inv = invert_factor(s_ref[lo - base : hi - base, lo - base : hi - base])
    w_ref[lo:hi, lo:hi] = inv
    if k:
        w_ref[lo:hi, :lo] = mm(inv, w_ref[lo:hi, :lo])
    if hi < N:
        u = mm(inv, s_ref[lo - base : hi - base, hi - base :])
        for q in range(k + 1, STEPS):
            a, b = q * B, (q + 1) * B
            uq = u[:, a - hi : b - hi]
            at = slice(a - base, b - base)
            s_ref[at, a - base :] = s_ref[at, a - base :] - mm_t(uq, u[:, a - hi :])
            w_ref[a:b, :hi] = w_ref[a:b, :hi] - mm_t(uq, w_ref[lo:hi, :hi])


def first_kernel(a_ref, s_out, w_ref, s_ref):
    for k in range(BANDS):
        band = a_ref[k * B : (k + 1) * B, :].astype(jnp.float32)
        j = STEPS - 1 - k
        s_ref[k * B : (k + 1) * B, k * B :] = band[:, : N - k * B]
        s_ref[j * B : (j + 1) * B, j * B :] = band[:, N - k * B :]
    w_ref[...] = jnp.zeros_like(w_ref)
    for k in range(SPLIT):
        eliminate(k, s_ref, w_ref, 0)
    s_out[...] = s_ref[CUT:, CUT:]


def second_kernel(s_in, w_in, hi_ref, lo_ref, s_ref, w_ref):
    s_ref[...] = s_in[...]
    w_ref[...] = w_in[...]
    for k in range(SPLIT, STEPS):
        eliminate(k, s_ref, w_ref, CUT)
    w = w_ref[...]
    high = w.astype(jnp.bfloat16)
    hi_ref[...] = high
    lo_ref[...] = (w - high.astype(jnp.float32)).astype(jnp.bfloat16)


def factor(folded):
    vm = pl.BlockSpec(memory_space=pltpu.VMEM)
    f32 = jnp.float32
    cost = pl.CostEstimate(flops=20_000_000_000, bytes_accessed=4_000_000, transcendentals=0)
    params = pltpu.CompilerParams(vmem_limit_bytes=16 << 20)
    rest = N - CUT
    state = pl.pallas_call(
        first_kernel,
        out_shape=[jax.ShapeDtypeStruct((rest, rest), f32), jax.ShapeDtypeStruct((N, N), f32)],
        in_specs=[vm],
        out_specs=[vm, vm],
        scratch_shapes=[pltpu.VMEM((N, N), f32)],
        compiler_params=params,
        cost_estimate=cost,
        name="factor_first",
    )(folded)
    return state, lambda s, w: pl.pallas_call(
        second_kernel,
        out_shape=[jax.ShapeDtypeStruct((N, N), jnp.bfloat16)] * 2,
        in_specs=[vm, vm],
        out_specs=[vm, vm],
        scratch_shapes=[pltpu.VMEM((rest, rest), f32), pltpu.VMEM((N, N), f32)],
        compiler_params=params,
        cost_estimate=cost,
        name="factor_second",
    )(s, w)


TILE = 256
PANEL = 256


def update_kernel(where_ref, cov_ref, rows_ref, cols_ref, hi_ref, lo_ref, out_ref, left_ref):
    row, col = where_ref[0], where_ref[1]
    step = pl.program_id(0)

    @pl.when(step == 0)
    def _():
        for k in range(N // PANEL):
            lo, hi = k * PANEL, (k + 1) * PANEL
            part = jnp.zeros((rows_ref.shape[0], PANEL), jnp.float32)
            for w_ref in (hi_ref, lo_ref):
                part += lax.dot_general(
                    rows_ref[:, :hi],
                    w_ref[lo:hi, :hi],
                    (((1,), (1,)), ((), ())),
                    preferred_element_type=jnp.float32,
                )
            left_ref[:, lo:hi] = part.astype(jnp.bfloat16)

    half = lax.div(step, N // TILE)
    panel = cols_ref[...]
    parts = []
    for k in range(N // PANEL):
        lo, hi = k * PANEL, (k + 1) * PANEL
        part = jnp.dot(hi_ref[lo:hi, :hi], panel[:hi], preferred_element_type=jnp.float32)
        part += jnp.dot(lo_ref[lo:hi, :hi], panel[:hi], preferred_element_type=jnp.float32)
        parts.append(part.astype(jnp.bfloat16))
    right = jnp.concatenate(parts, axis=0)
    product = jnp.dot(left_ref[...], right, preferred_element_type=jnp.float32)
    value = (cov_ref[...].astype(jnp.float32) - product).astype(jnp.bfloat16)
    keep = jnp.logical_and(row > 0, jnp.logical_or(col > 0, half > 0))
    out_ref[...] = jnp.where(keep, value, jnp.zeros_like(value))


def update(place, cov, rows, cols, hi, lo):
    n_rows, n_cols = cov.shape
    vm = pl.BlockSpec(memory_space=pltpu.VMEM)
    tile = pl.BlockSpec((n_rows, TILE), lambda j: (0, j))
    return pl.pallas_call(
        update_kernel,
        out_shape=jax.ShapeDtypeStruct(cov.shape, jnp.bfloat16),
        grid=(n_cols // TILE,),
        in_specs=[pl.BlockSpec(memory_space=pltpu.SMEM), tile, vm, pl.BlockSpec((N, TILE), lambda j: (0, j)), vm, vm],
        out_specs=tile,
        scratch_shapes=[pltpu.VMEM((n_rows, N), jnp.bfloat16)],
        compiler_params=pltpu.CompilerParams(vmem_limit_bytes=24 << 20),
        name="update",
    )(place, cov, rows, cols, hi, lo)


DEPTH = 8
PART = N // 4
AXES = ("row", "col")


def device(x, y, z, core):
    return ((x % 4 * 4 + y % 4) * 2 + core) * 2 * DEPTH + (y % 8 // 4) * DEPTH + z % DEPTH


def send(x, pairs):
    return lax.ppermute(x, AXES, pairs)


def chips(xs, ys, zs):
    return [(x, y, z) for x in xs for y in ys for z in zs]


def shifts(sources, by, cores=(0,)):
    return [
        (device(x, y, z, c), device(x + by[0], y + by[1], z + by[2], c)) for x, y, z in sources for c in cores
    ]


def fan(x, sources, offsets, cores=(0,)):
    return sum([send(x, shifts(sources, by, cores)) for by in offsets], x)


def scatter(x, size, sources, offsets, cores=(0,)):
    sent = [
        send(x[i * size : (i + 1) * size], shifts(sources, by, cores)) for i, by in enumerate(offsets, 1)
    ]
    return sum(sent, x[:size])


def per_device(covariance):
    row = lax.axis_index("row")
    col = lax.axis_index("col")
    place = jnp.stack([row, col]).astype(jnp.int32)

    leading = jnp.where(jnp.logical_and(row == 0, col == 0), fold(covariance[:, :N]), 0)
    along_x = [(1, 0, 0), (2, 0, 0), (3, 0, 0)]
    leading = scatter(leading, leading.shape[0] // 4, [(0, 0, 0)], along_x)
    leading = fan(leading, chips(range(4), [0], [0]), [(0, 0, 4), (0, 0, 2), (0, 0, 6)])
    leading = fan(leading, chips(range(4), [0], range(0, 8, 2)), [(0, 4, 1), (0, 4, 0), (0, 0, 1)])
    leading = fan(leading, chips(range(4), [0, 4], range(8)), [(0, 2, 0), (0, 1, 0), (0, 7, 0)])
    leading = leading + lax.ppermute(leading, "row", [(2 * chip, 2 * chip + 1) for chip in range(16)])
    same_x = [[8 * x + i for x in range(4)] for i in range(8)]
    leading = lax.all_gather(leading, "row", axis=0, tiled=True, axis_index_groups=same_x)

    columns = chips([0], [0, 4], range(8))
    cols = jnp.where(row == 0, covariance, 0)
    cols = scatter(cols, PART, columns, along_x)
    cols = scatter(cols, PART // 4, chips(range(4), [0, 4], range(8)), [(0, 1, 0), (0, 2, 0), (0, 3, 0)])
    half = cols.shape[0] // 2
    other = lax.ppermute(cols[half:], "row", [(2 * chip, 2 * chip + 1) for chip in range(16)])
    cols = jnp.where(row % 2 == 0, cols[:half], other)
    cols = lax.all_gather(cols, "row", axis=0, tiled=True)

    both = (0, 1)
    rows = jnp.where(col == 0, covariance[:, :N], 0)
    rows = scatter(rows, PART, chips(range(4), range(4), [0]), [(0, 0, 2), (0, 0, 4), (0, 0, 6)], both)
    rows = fan(rows, chips(range(4), range(4), range(0, 8, 2)), [(0, 0, 1)], both)
    rows = fan(rows, chips(range(4), range(4), range(8)), [(0, 4, 0)], both)
    same_z = [[8 * y + odd + 2 * z for z in range(4)] for y in range(2) for odd in range(2)]
    copies = jnp.broadcast_to(rows[None], (4, *rows.shape)).reshape(N, N)

    (s, w), finish = factor(leading)
    rows = lax.all_to_all(copies, "col", 0, 0, axis_index_groups=same_z, tiled=True)
    hi, lo = finish(s, w)
    return update(place, covariance, rows, cols, hi, lo)


def solution(mesh):
    return jax.shard_map(
        per_device,
        mesh=mesh,
        in_specs=(P("row", "col"),),
        out_specs=P("row", "col"),
        check_vma=False,
    )
```

```python
import jax
import jax.numpy as jnp
from jax import lax
from jax.experimental import pallas as pl
from jax.experimental.pallas import tpu as pltpu
from jax.sharding import PartitionSpec as P

N = 768
B = 128
STEPS = N // B
HI = lax.Precision.HIGHEST


def mm(a, b):
    return jnp.dot(a, b, precision=HI, preferred_element_type=jnp.float32)


def mm_t(a, b):
    return lax.dot_general(
        a, b, (((0,), (0,)), ((), ())), precision=HI, preferred_element_type=jnp.float32
    )


def invert_factor(block):
    groups = B // 8
    lane = lax.broadcasted_iota(jnp.int32, (8, B), 1)
    sub = lax.broadcasted_iota(jnp.int32, (8, B), 0)
    left = [block[8 * g : 8 * g + 8] for g in range(groups)]
    right = [jnp.where(lane == sub + 8 * g, 1.0, 0.0).astype(jnp.float32) for g in range(groups)]
    done = []

    def over_rows(x, i):
        return jnp.broadcast_to(x[i : i + 1], (8, B))

    def over_lanes(x, i):
        return jnp.broadcast_to(x[:, i : i + 1], (8, B))

    for g in range(groups):
        first = 8 * g
        last = g == groups - 1
        row_l, row_r = left[g], right[g]
        own = [over_lanes(row_l, first + i) for i in range(8)]
        if not last:
            nxt_l, nxt_r = left[g + 1], right[g + 1]
            nxt = [over_lanes(nxt_l, first + i) for i in range(8)]
        pivot = jnp.ones((8, B), jnp.float32)
        for i in range(8):
            d = over_rows(own[i], i)
            r = 1.0 / d
            pivot = jnp.where(sub == i, d, pivot)
            m = jnp.where(sub > i, own[i] * r, 0.0)
            rows = [over_rows(own[t], i) for t in range(i + 1, 8)]
            for t in range(i + 1, 8):
                own[t] = own[t] - m * rows[t - i - 1]
            rl, rr = over_rows(row_l, i), over_rows(row_r, i)
            row_l = row_l - m * rl
            row_r = row_r - m * rr
            if not last:
                n = nxt[i] * r
                for t in range(i + 1, 8):
                    nxt[t] = nxt[t] - n * rows[t - i - 1]
                nxt_l = nxt_l - n * rl
                nxt_r = nxt_r - n * rr
        scale = lax.rsqrt(pivot)
        done.append(row_r * scale)
        if not last:
            left[g + 1], right[g + 1] = nxt_l, nxt_r
        if g + 2 < groups:
            ul = row_l * scale
            cut = jnp.where(lane >= first + 16, ul, 0.0)
            both = mm_t(cut, jnp.concatenate([ul, row_r * scale], axis=1))
            for q in range(g + 2, groups):
                left[q] = left[q] - both[8 * q : 8 * q + 8, :B]
                right[q] = right[q] - both[8 * q : 8 * q + 8, B:]
    return jnp.concatenate(done, axis=0)


BANDS = STEPS // 2
FOLD = (STEPS + 1) * B
FOLD_ROWS = BANDS * B
SPLIT = 3
CUT = SPLIT * B


def prepare_kernel(where_ref, cov_ref, low_ref, high_ref, rows_low_ref, rows_high_ref):
    row, col = where_ref[0], where_ref[1]
    own = jnp.logical_and(row == 0, col == 0)
    zero = jnp.zeros((), cov_ref.dtype)
    half = FOLD_ROWS // 2
    for k in range(STEPS):
        j = min(k, STEPS - 1 - k)
        at = slice(0, N - k * B) if j == k else slice(N - j * B, FOLD)
        for first in range(0, B, B // 2):
            to = j * B + first
            ref, to = (low_ref, to) if to < half else (high_ref, to - half)
            rows = slice(k * B + first, k * B + first + B // 2)
            ref[to : to + B // 2, at] = jnp.where(own, cov_ref[rows, k * B : N], zero)
    rows_low_ref[...] = jnp.where(col == 0, cov_ref[: N // 2, :N], zero)
    rows_high_ref[...] = jnp.where(col == 0, cov_ref[N // 2 :, :N], zero)


def prepare(place, cov):
    vm = pl.BlockSpec(memory_space=pltpu.VMEM)
    folded = pltpu.VMEM((FOLD_ROWS // 2, FOLD), cov.dtype)
    rows = pltpu.HBM((N // 2, N), cov.dtype)
    return pl.pallas_call(
        prepare_kernel,
        out_shape=[folded, folded, rows, rows],
        in_specs=[pl.BlockSpec(memory_space=pltpu.SMEM), vm],
        out_specs=[vm, vm, vm, vm],
        compiler_params=pltpu.CompilerParams(vmem_limit_bytes=16 << 20),
        name="prepare",
    )(place, cov)


def eliminate(k, s_ref, w_ref, base):
    lo, hi = k * B, (k + 1) * B
    inv = invert_factor(s_ref[lo - base : hi - base, lo - base : hi - base])
    w_ref[lo:hi, lo:hi] = inv
    if k:
        w_ref[lo:hi, :lo] = mm(inv, w_ref[lo:hi, :lo])
    if hi < N:
        u = mm(inv, s_ref[lo - base : hi - base, hi - base :])
        for q in range(k + 1, STEPS):
            a, b = q * B, (q + 1) * B
            uq = u[:, a - hi : b - hi]
            at = slice(a - base, b - base)
            s_ref[at, a - base :] = s_ref[at, a - base :] - mm_t(uq, u[:, a - hi :])
            w_ref[a:b, :hi] = w_ref[a:b, :hi] - mm_t(uq, w_ref[lo:hi, :hi])


def write_out(pairs, sem):
    copies = [pltpu.make_async_copy(src, dst, sem.at[i]) for i, (src, dst) in enumerate(pairs)]
    for copy in copies:
        copy.start()
    for copy in copies:
        copy.wait()


def first_kernel(a_ref, s_out, w_out, s_ref, w_ref, sem):
    for k in range(BANDS):
        band = a_ref[k * B : (k + 1) * B, :].astype(jnp.float32)
        j = STEPS - 1 - k
        s_ref[k * B : (k + 1) * B, k * B :] = band[:, : N - k * B]
        s_ref[j * B : (j + 1) * B, j * B :] = band[:, N - k * B :]
    w_ref[...] = jnp.zeros_like(w_ref)
    for k in range(SPLIT):
        eliminate(k, s_ref, w_ref, 0)
    write_out([(s_ref.at[CUT:, CUT:], s_out), (w_ref, w_out)], sem)


def second_kernel(s_in, w_in, hi_out, lo_out, s_ref, w_ref, hi_ref, lo_ref, sem):
    s_ref[...] = s_in[...]
    w_ref[...] = w_in[...]
    for k in range(SPLIT, STEPS):
        eliminate(k, s_ref, w_ref, CUT)
    w = w_ref[...]
    high = w.astype(jnp.bfloat16)
    hi_ref[...] = high
    lo_ref[...] = (w - high.astype(jnp.float32)).astype(jnp.bfloat16)
    write_out([(hi_ref, hi_out), (lo_ref, lo_out)], sem)


def factor(folded):
    vm = pl.BlockSpec(memory_space=pltpu.VMEM)
    hbm = pl.BlockSpec(memory_space=pltpu.HBM)
    sems = pltpu.SemaphoreType.DMA((2,))
    low = pltpu.VMEM((N, N), jnp.bfloat16)
    f32 = jnp.float32
    cost = pl.CostEstimate(flops=20_000_000_000, bytes_accessed=4_000_000, transcendentals=0)
    params = pltpu.CompilerParams(vmem_limit_bytes=16 << 20)
    rest = N - CUT
    state = pl.pallas_call(
        first_kernel,
        out_shape=[pltpu.HBM((rest, rest), f32), pltpu.HBM((N, N), f32)],
        in_specs=[vm],
        out_specs=[hbm, hbm],
        scratch_shapes=[pltpu.VMEM((N, N), f32), pltpu.VMEM((N, N), f32), sems],
        compiler_params=params,
        cost_estimate=cost,
        name="factor_first",
    )(folded)
    return state, lambda s, w: pl.pallas_call(
        second_kernel,
        out_shape=[pltpu.HBM((N, N), jnp.bfloat16)] * 2,
        in_specs=[vm, vm],
        out_specs=[hbm, hbm],
        scratch_shapes=[pltpu.VMEM((rest, rest), f32), pltpu.VMEM((N, N), f32), low, low, sems],
        compiler_params=params,
        cost_estimate=cost,
        name="factor_second",
    )(s, w)


TILE = 256
PANEL = 256


def update_kernel(where_ref, cov_ref, rows_ref, cols_ref, hi_ref, lo_ref, out_ref, left_ref):
    row, col = where_ref[0], where_ref[1]
    step = pl.program_id(0)

    @pl.when(step == 0)
    def _():
        for k in range(N // PANEL):
            lo, hi = k * PANEL, (k + 1) * PANEL
            part = jnp.zeros((rows_ref.shape[0], PANEL), jnp.float32)
            for w_ref in (hi_ref, lo_ref):
                part += lax.dot_general(
                    rows_ref[:, :hi],
                    w_ref[lo:hi, :hi],
                    (((1,), (1,)), ((), ())),
                    preferred_element_type=jnp.float32,
                )
            left_ref[:, lo:hi] = part.astype(jnp.bfloat16)

    half = lax.div(step, N // TILE)
    panel = cols_ref[...]
    parts = []
    for k in range(N // PANEL):
        lo, hi = k * PANEL, (k + 1) * PANEL
        part = jnp.dot(hi_ref[lo:hi, :hi], panel[:hi], preferred_element_type=jnp.float32)
        part += jnp.dot(lo_ref[lo:hi, :hi], panel[:hi], preferred_element_type=jnp.float32)
        parts.append(part.astype(jnp.bfloat16))
    right = jnp.concatenate(parts, axis=0)
    product = jnp.dot(left_ref[...], right, preferred_element_type=jnp.float32)
    value = (cov_ref[...].astype(jnp.float32) - product).astype(jnp.bfloat16)
    keep = jnp.logical_and(row > 0, jnp.logical_or(col > 0, half > 0))
    out_ref[...] = jnp.where(keep, value, jnp.zeros_like(value))


def update(place, cov, rows, cols, hi, lo):
    n_rows, n_cols = cov.shape
    vm = pl.BlockSpec(memory_space=pltpu.VMEM)
    tile = pl.BlockSpec((n_rows, TILE), lambda j: (0, j))
    return pl.pallas_call(
        update_kernel,
        out_shape=jax.ShapeDtypeStruct(cov.shape, jnp.bfloat16),
        grid=(n_cols // TILE,),
        in_specs=[pl.BlockSpec(memory_space=pltpu.SMEM), tile, vm, pl.BlockSpec((N, TILE), lambda j: (0, j)), vm, vm],
        out_specs=tile,
        scratch_shapes=[pltpu.VMEM((n_rows, N), jnp.bfloat16)],
        compiler_params=pltpu.CompilerParams(vmem_limit_bytes=24 << 20),
        name="update",
    )(place, cov, rows, cols, hi, lo)


DEPTH = 8
PART = N // 4
AXES = ("row", "col")


def device(x, y, z, core):
    return ((x % 4 * 4 + y % 4) * 2 + core) * 2 * DEPTH + (y % 8 // 4) * DEPTH + z % DEPTH


def send(x, pairs):
    return lax.ppermute(x, AXES, pairs)


def chips(xs, ys, zs):
    return [(x, y, z) for x in xs for y in ys for z in zs]


def shifts(sources, by, cores=(0,)):
    return [
        (device(x, y, z, c), device(x + by[0], y + by[1], z + by[2], c)) for x, y, z in sources for c in cores
    ]


def halve(low, high, sources, by, cores=(0,)):
    return low + send(high, shifts(sources, by, cores))


def halves(x):
    return x[: x.shape[0] // 2], x[x.shape[0] // 2 :]


def double(x, sources, by, cores=(0,)):
    return x + send(x, shifts(sources, by, cores))


def other_core(x):
    return x + lax.ppermute(x, "row", [(2 * chip, 2 * chip + 1) for chip in range(16)])


def gather(x, axis, groups):
    copies = jnp.broadcast_to(x[None], (4, *x.shape)).reshape(4 * x.shape[0], x.shape[1])
    return lax.all_to_all(copies, axis, 0, 0, axis_index_groups=groups, tiled=True)


SAME_X = [[8 * x + i for x in range(4)] for i in range(8)]
SAME_Z = [[8 * y + odd + 2 * z for z in range(4)] for y in range(2) for odd in range(2)]


def per_device(covariance):
    row = lax.axis_index("row")
    col = lax.axis_index("col")
    place = jnp.stack([row, col]).astype(jnp.int32)
    both = (0, 1)
    all_x, even_z, all_z = range(4), range(0, 8, 2), range(8)
    low, high, rows_low, rows_high = prepare(place, covariance)

    together = lambda *arrays: lax.optimization_barrier(arrays)
    lead = halve(low, high, [(0, 0, 0)], (2, 0, 0))
    rows = halve(rows_low, rows_high, chips(all_x, range(4), [0]), (0, 0, 4), both)
    lead, covariance_late = together(lead, covariance)
    cols = jnp.where(row == 0, covariance_late, 0)
    lead = halve(*halves(lead), chips([0, 2], [0], [0]), (1, 0, 0))
    cols = halve(*halves(cols), chips([0], [0, 4], all_z), (2, 0, 0))
    lead = double(lead, chips(all_x, [0], [0]), (0, 4, 0))
    lead, rows = together(lead, rows)
    rows = halve(*halves(rows), chips(all_x, range(4), [0, 4]), (0, 0, 2), both)
    lead = double(lead, chips(all_x, [0, 4], [0]), (0, 2, 0))
    lead, cols = together(lead, cols)
    cols = halve(*halves(cols), chips([0, 2], [0, 4], all_z), (1, 0, 0))
    lead = double(lead, chips(all_x, even_z, [0]), (0, 1, 0))
    lead, rows = together(lead, rows)
    rows = double(rows, chips(all_x, range(4), even_z), (0, 0, 1), both)
    lead = double(lead, chips(all_x, all_z, [0]), (0, 0, 4))
    lead, cols = together(lead, cols)
    cols = double(cols, chips(all_x, [0, 4], all_z), (0, 2, 0))
    lead = double(lead, chips(all_x, all_z, [0, 4]), (0, 0, 2))
    lead, rows = together(lead, rows)
    rows = double(rows, chips(all_x, range(4), all_z), (0, 4, 0), both)
    lead = double(lead, chips(all_x, all_z, even_z), (0, 0, 1))
    lead, cols = together(lead, cols)
    cols = double(cols, chips(all_x, [0, 2, 4, 6], all_z), (0, 1, 0))
    lead = gather(other_core(lead), "row", SAME_X)
    lead, cols = together(lead, cols)
    cols = other_core(cols)

    (s, w), finish = factor(lead)
    s, rows, cols = together(s, rows, cols)
    rows = gather(rows, "col", SAME_Z)
    cols = gather(cols, "row", SAME_X)
    hi, lo = finish(s, w)
    return update(place, covariance, rows, cols, hi, lo)


def solution(mesh):
    return jax.shard_map(
        per_device,
        mesh=mesh,
        in_specs=(P("row", "col"),),
        out_specs=P("row", "col"),
        check_vma=False,
    )
```

```python
import jax
import jax.numpy as jnp
from jax import lax
from jax.experimental import pallas as pl
from jax.experimental.pallas import tpu as pltpu
from jax.sharding import PartitionSpec as P

N = 768
B = 128
STEPS = N // B
HI = lax.Precision.HIGHEST


def mm(a, b):
    return jnp.dot(a, b, precision=HI, preferred_element_type=jnp.float32)


def mm_t(a, b):
    return lax.dot_general(
        a, b, (((0,), (0,)), ((), ())), precision=HI, preferred_element_type=jnp.float32
    )


def invert_factor(block):
    groups = B // 8
    lane = lax.broadcasted_iota(jnp.int32, (8, B), 1)
    sub = lax.broadcasted_iota(jnp.int32, (8, B), 0)
    left = [block[8 * g : 8 * g + 8] for g in range(groups)]
    right = [jnp.where(lane == sub + 8 * g, 1.0, 0.0).astype(jnp.float32) for g in range(groups)]
    done = []

    def over_rows(x, i):
        return jnp.broadcast_to(x[i : i + 1], (8, B))

    def over_lanes(x, i):
        return jnp.broadcast_to(x[:, i : i + 1], (8, B))

    for g in range(groups):
        first = 8 * g
        last = g == groups - 1
        row_l, row_r = left[g], right[g]
        own = [over_lanes(row_l, first + i) for i in range(8)]
        if not last:
            nxt_l, nxt_r = left[g + 1], right[g + 1]
            nxt = [over_lanes(nxt_l, first + i) for i in range(8)]
        pivot = jnp.ones((8, B), jnp.float32)
        for i in range(8):
            d = over_rows(own[i], i)
            r = 1.0 / d
            pivot = jnp.where(sub == i, d, pivot)
            m = jnp.where(sub > i, own[i] * r, 0.0)
            rows = [over_rows(own[t], i) for t in range(i + 1, 8)]
            for t in range(i + 1, 8):
                own[t] = own[t] - m * rows[t - i - 1]
            rl, rr = over_rows(row_l, i), over_rows(row_r, i)
            row_l = row_l - m * rl
            row_r = row_r - m * rr
            if not last:
                n = nxt[i] * r
                for t in range(i + 1, 8):
                    nxt[t] = nxt[t] - n * rows[t - i - 1]
                nxt_l = nxt_l - n * rl
                nxt_r = nxt_r - n * rr
        scale = lax.rsqrt(pivot)
        done.append(row_r * scale)
        if not last:
            left[g + 1], right[g + 1] = nxt_l, nxt_r
        if g + 2 < groups:
            ul = row_l * scale
            cut = jnp.where(lane >= first + 16, ul, 0.0)
            both = mm_t(cut, jnp.concatenate([ul, row_r * scale], axis=1))
            for q in range(g + 2, groups):
                left[q] = left[q] - both[8 * q : 8 * q + 8, :B]
                right[q] = right[q] - both[8 * q : 8 * q + 8, B:]
    return jnp.concatenate(done, axis=0)


BANDS = STEPS // 2
FOLD = (STEPS + 1) * B
FOLD_ROWS = BANDS * B


def prepare_kernel(where_ref, cov_ref, low_ref, high_ref, rows_low_ref, rows_high_ref):
    row, col = where_ref[0], where_ref[1]
    own = jnp.logical_and(row == 0, col == 0)
    zero = jnp.zeros((), cov_ref.dtype)
    half = FOLD_ROWS // 2
    for k in range(STEPS):
        j = min(k, STEPS - 1 - k)
        at = slice(0, N - k * B) if j == k else slice(N - j * B, FOLD)
        for first in range(0, B, B // 2):
            to = j * B + first
            ref, to = (low_ref, to) if to < half else (high_ref, to - half)
            rows = slice(k * B + first, k * B + first + B // 2)
            ref[to : to + B // 2, at] = jnp.where(own, cov_ref[rows, k * B : N], zero)
    rows_low_ref[...] = jnp.where(col == 0, cov_ref[: N // 2, :N], zero)
    rows_high_ref[...] = jnp.where(col == 0, cov_ref[N // 2 :, :N], zero)


def prepare(place, cov):
    vm = pl.BlockSpec(memory_space=pltpu.VMEM)
    folded = pltpu.VMEM((FOLD_ROWS // 2, FOLD), cov.dtype)
    rows = pltpu.HBM((N // 2, N), cov.dtype)
    return pl.pallas_call(
        prepare_kernel,
        out_shape=[folded, folded, rows, rows],
        in_specs=[pl.BlockSpec(memory_space=pltpu.SMEM), vm],
        out_specs=[vm, vm, vm, vm],
        compiler_params=pltpu.CompilerParams(vmem_limit_bytes=16 << 20),
        name="prepare",
    )(place, cov)


def eliminate(k, s_ref, w_ref, base):
    lo, hi = k * B, (k + 1) * B
    inv = invert_factor(s_ref[lo - base : hi - base, lo - base : hi - base])
    w_ref[lo:hi, lo:hi] = inv
    if k:
        w_ref[lo:hi, :lo] = mm(inv, w_ref[lo:hi, :lo])
    if hi < N:
        u = mm(inv, s_ref[lo - base : hi - base, hi - base :])
        for q in range(k + 1, STEPS):
            a, b = q * B, (q + 1) * B
            uq = u[:, a - hi : b - hi]
            at = slice(a - base, b - base)
            s_ref[at, a - base :] = s_ref[at, a - base :] - mm_t(uq, u[:, a - hi :])
            w_ref[a:b, :hi] = w_ref[a:b, :hi] - mm_t(uq, w_ref[lo:hi, :hi])


def write_out(pairs, sem):
    copies = [pltpu.make_async_copy(src, dst, sem.at[i]) for i, (src, dst) in enumerate(pairs)]
    for copy in copies:
        copy.start()
    for copy in copies:
        copy.wait()


def factor_kernel(a_ref, hi_out, lo_out, s_ref, w_ref, hi_ref, lo_ref, sem):
    for k in range(BANDS):
        band = a_ref[k * B : (k + 1) * B, :].astype(jnp.float32)
        j = STEPS - 1 - k
        s_ref[k * B : (k + 1) * B, k * B :] = band[:, : N - k * B]
        s_ref[j * B : (j + 1) * B, j * B :] = band[:, N - k * B :]
    w_ref[...] = jnp.zeros_like(w_ref)
    for k in range(STEPS):
        eliminate(k, s_ref, w_ref, 0)
    w = w_ref[...]
    high = w.astype(jnp.bfloat16)
    hi_ref[...] = high
    lo_ref[...] = (w - high.astype(jnp.float32)).astype(jnp.bfloat16)
    write_out([(hi_ref, hi_out), (lo_ref, lo_out)], sem)


def factor(folded):
    vm = pl.BlockSpec(memory_space=pltpu.VMEM)
    hbm = pl.BlockSpec(memory_space=pltpu.HBM)
    f32, low = pltpu.VMEM((N, N), jnp.float32), pltpu.VMEM((N, N), jnp.bfloat16)
    return pl.pallas_call(
        factor_kernel,
        out_shape=[pltpu.HBM((N, N), jnp.bfloat16)] * 2,
        in_specs=[vm],
        out_specs=[hbm, hbm],
        scratch_shapes=[f32, f32, low, low, pltpu.SemaphoreType.DMA((2,))],
        compiler_params=pltpu.CompilerParams(vmem_limit_bytes=16 << 20),
        cost_estimate=pl.CostEstimate(flops=40_000_000_000, bytes_accessed=4_000_000, transcendentals=0),
        name="factor",
    )(folded)


TILE = 256
PANEL = 256


def update_kernel(where_ref, cov_ref, rows_ref, cols_ref, hi_ref, lo_ref, out_ref, left_ref):
    row, col = where_ref[0], where_ref[1]
    step = pl.program_id(0)

    @pl.when(step == 0)
    def _():
        for k in range(N // PANEL):
            lo, hi = k * PANEL, (k + 1) * PANEL
            part = jnp.zeros((rows_ref.shape[0], PANEL), jnp.float32)
            for w_ref in (hi_ref, lo_ref):
                part += lax.dot_general(
                    rows_ref[:, :hi],
                    w_ref[lo:hi, :hi],
                    (((1,), (1,)), ((), ())),
                    preferred_element_type=jnp.float32,
                )
            left_ref[:, lo:hi] = part.astype(jnp.bfloat16)

    half = lax.div(step, N // TILE)
    panel = cols_ref[...]
    parts = []
    for k in range(N // PANEL):
        lo, hi = k * PANEL, (k + 1) * PANEL
        part = jnp.dot(hi_ref[lo:hi, :hi], panel[:hi], preferred_element_type=jnp.float32)
        part += jnp.dot(lo_ref[lo:hi, :hi], panel[:hi], preferred_element_type=jnp.float32)
        parts.append(part.astype(jnp.bfloat16))
    right = jnp.concatenate(parts, axis=0)
    product = jnp.dot(left_ref[...], right, preferred_element_type=jnp.float32)
    value = (cov_ref[...].astype(jnp.float32) - product).astype(jnp.bfloat16)
    keep = jnp.logical_and(row > 0, jnp.logical_or(col > 0, half > 0))
    out_ref[...] = jnp.where(keep, value, jnp.zeros_like(value))


def update(place, cov, rows, cols, hi, lo):
    n_rows, n_cols = cov.shape
    vm = pl.BlockSpec(memory_space=pltpu.VMEM)
    tile = pl.BlockSpec((n_rows, TILE), lambda j: (0, j))
    return pl.pallas_call(
        update_kernel,
        out_shape=jax.ShapeDtypeStruct(cov.shape, jnp.bfloat16),
        grid=(n_cols // TILE,),
        in_specs=[pl.BlockSpec(memory_space=pltpu.SMEM), tile, vm, pl.BlockSpec((N, TILE), lambda j: (0, j)), vm, vm],
        out_specs=tile,
        scratch_shapes=[pltpu.VMEM((n_rows, N), jnp.bfloat16)],
        compiler_params=pltpu.CompilerParams(vmem_limit_bytes=24 << 20),
        name="update",
    )(place, cov, rows, cols, hi, lo)


DEPTH = 8
PART = N // 4
AXES = ("row", "col")


def device(x, y, z, core):
    return ((x % 4 * 4 + y % 4) * 2 + core) * 2 * DEPTH + (y % 8 // 4) * DEPTH + z % DEPTH


def send(x, pairs):
    return lax.ppermute(x, AXES, pairs)


def chips(xs, ys, zs):
    return [(x, y, z) for x in xs for y in ys for z in zs]


def shifts(sources, by, cores=(0,)):
    return [
        (device(x, y, z, c), device(x + by[0], y + by[1], z + by[2], c)) for x, y, z in sources for c in cores
    ]


def halve(low, high, sources, by, cores=(0,)):
    return low + send(high, shifts(sources, by, cores))


def halves(x):
    return x[: x.shape[0] // 2], x[x.shape[0] // 2 :]


def double(x, sources, by, cores=(0,)):
    return x + send(x, shifts(sources, by, cores))


def gather(x, axis, groups):
    copies = jnp.broadcast_to(x[None], (4, *x.shape)).reshape(4 * x.shape[0], x.shape[1])
    return lax.all_to_all(copies, axis, 0, 0, axis_index_groups=groups, tiled=True)


SAME_X = [[8 * x + i for x in range(4)] for i in range(8)]
SAME_Z = [[8 * y + odd + 2 * z for z in range(4)] for y in range(2) for odd in range(2)]


def per_device(covariance):
    row = lax.axis_index("row")
    col = lax.axis_index("col")
    place = jnp.stack([row, col]).astype(jnp.int32)
    both = (0, 1)
    all_x, even_z, all_z = range(4), range(0, 8, 2), range(8)
    low, high, rows_low, rows_high = prepare(place, covariance)

    together = lambda *arrays: lax.optimization_barrier(arrays)
    lead = halve(low, high, [(0, 0, 0)], (2, 0, 0))
    rows = halve(rows_low, rows_high, chips(all_x, range(4), [0]), (0, 0, 4), both)
    lead = halve(*halves(lead), chips([0, 2], [0], [0]), (1, 0, 0))
    lead, covariance_late = together(lead, covariance)
    cols = jnp.where(row == 0, covariance_late, 0)
    cols = halve(*halves(cols), chips([0], [0, 4], all_z), (2, 0, 0))
    lead = double(lead, chips(all_x, [0], [0]), (0, 4, 0))
    lead, rows = together(lead, rows)
    rows = halve(*halves(rows), chips(all_x, range(4), [0, 4]), (0, 0, 2), both)
    lead = double(lead, chips(all_x, [0, 4], [0]), (0, 2, 0))
    lead = double(lead, chips(all_x, even_z, [0]), (0, 1, 0))
    lead, cols = together(lead, cols)
    cols = halve(*halves(cols), chips([0, 2], [0, 4], all_z), (1, 0, 0))
    lead, rows = together(lead, rows)
    rows = double(rows, chips(all_x, range(4), even_z), (0, 0, 1), both)
    lead = double(lead, chips(all_x, all_z, [0]), (0, 0, 4))
    lead, cols = together(lead, cols)
    cols = halve(*halves(cols), chips(all_x, [0, 4], all_z), (0, 2, 0))
    lead, rows = together(lead, rows)
    rows = double(rows, chips(all_x, range(4), all_z), (0, 4, 0), both)
    lead = double(lead, chips(all_x, all_z, [0, 4]), (0, 0, 2))
    lead, cols = together(lead, cols)
    cols = halve(*halves(cols), chips(all_x, even_z, all_z), (0, 1, 0))
    lead = double(lead, chips(all_x, all_z, even_z), (0, 0, 1))
    lead, cols = together(lead, cols)
    kept, passed = halves(cols)
    pairs = [(2 * chip, 2 * chip + 1) for chip in range(16)]
    cols = jnp.where(row % 2 == 0, kept, lax.ppermute(passed, "row", pairs))
    lead = lead + lax.ppermute(lead, "row", pairs)
    lead, rows, cols = together(lead, rows, cols)
    cols = lax.all_gather(cols, "row", axis=0, tiled=True)
    lead = gather(lead, "row", SAME_X)
    rows = gather(rows, "col", SAME_Z)
    hi, lo = factor(lead)
    return update(place, covariance, rows, cols, hi, lo)


def solution(mesh):
    return jax.shard_map(
        per_device,
        mesh=mesh,
        in_specs=(P("row", "col"),),
        out_specs=P("row", "col"),
        check_vma=False,
    )
```

```python
import jax
import jax.numpy as jnp
from jax import lax
from jax.experimental import pallas as pl
from jax.experimental.pallas import tpu as pltpu
from jax.sharding import PartitionSpec as P

N = 768
B = 128
STEPS = N // B


def split(x):
    high = x.astype(jnp.bfloat16)
    return high, (x - high.astype(jnp.float32)).astype(jnp.bfloat16)


def product(a, b, dim):
    dot = lambda x, y: lax.dot_general(x, y, (((dim,), (0,)), ((), ())), preferred_element_type=jnp.float32)
    (a_high, a_low), (b_high, b_low) = split(a), split(b)
    return dot(a_high, b_high) + (dot(a_high, b_low) + dot(a_low, b_high))


def mm(a, b):
    return product(a, b, 1)


def mm_t(a, b):
    return product(a, b, 0)


def invert_factor(block):
    groups = B // 8
    lane = lax.broadcasted_iota(jnp.int32, (8, B), 1)
    sub = lax.broadcasted_iota(jnp.int32, (8, B), 0)
    left = [block[8 * g : 8 * g + 8] for g in range(groups)]
    right = [jnp.where(lane == sub + 8 * g, 1.0, 0.0).astype(jnp.float32) for g in range(groups)]
    done = []

    def over_rows(x, i):
        return jnp.broadcast_to(x[i : i + 1], (8, B))

    def over_lanes(x, i):
        return jnp.broadcast_to(x[:, i : i + 1], (8, B))

    for g in range(groups):
        first = 8 * g
        last = g == groups - 1
        row_l, row_r = left[g], right[g]
        own = [over_lanes(row_l, first + i) for i in range(8)]
        if not last:
            nxt_l, nxt_r = left[g + 1], right[g + 1]
            nxt = [over_lanes(nxt_l, first + i) for i in range(8)]
        pivot = jnp.ones((8, B), jnp.float32)
        for i in range(8):
            d = over_rows(own[i], i)
            r = 1.0 / d
            pivot = jnp.where(sub == i, d, pivot)
            m = jnp.where(sub > i, own[i] * r, 0.0)
            rows = [over_rows(own[t], i) for t in range(i + 1, 8)]
            for t in range(i + 1, 8):
                own[t] = own[t] - m * rows[t - i - 1]
            rl, rr = over_rows(row_l, i), over_rows(row_r, i)
            row_l = row_l - m * rl
            row_r = row_r - m * rr
            if not last:
                n = nxt[i] * r
                for t in range(i + 1, 8):
                    nxt[t] = nxt[t] - n * rows[t - i - 1]
                nxt_l = nxt_l - n * rl
                nxt_r = nxt_r - n * rr
        scale = lax.rsqrt(pivot)
        done.append(row_r * scale)
        if not last:
            left[g + 1], right[g + 1] = nxt_l, nxt_r
        if g + 2 < groups:
            ul = row_l * scale
            cut = jnp.where(lane >= first + 16, ul, 0.0)
            both = mm_t(cut, jnp.concatenate([ul, row_r * scale], axis=1))
            for q in range(g + 2, groups):
                left[q] = left[q] - both[8 * q : 8 * q + 8, :B]
                right[q] = right[q] - both[8 * q : 8 * q + 8, B:]
    return jnp.concatenate(done, axis=0)


BANDS = STEPS // 2
FOLD = (STEPS + 1) * B
FOLD_ROWS = BANDS * B


def prepare_kernel(where_ref, cov_ref, low_ref, high_ref, rows_low_ref, rows_high_ref):
    row, col = where_ref[0], where_ref[1]
    own = jnp.logical_and(row == 0, col == 0)
    zero = jnp.zeros((), cov_ref.dtype)
    half = FOLD_ROWS // 2
    for k in range(STEPS):
        j = min(k, STEPS - 1 - k)
        at = slice(0, N - k * B) if j == k else slice(N - j * B, FOLD)
        for first in range(0, B, B // 2):
            to = j * B + first
            ref, to = (low_ref, to) if to < half else (high_ref, to - half)
            rows = slice(k * B + first, k * B + first + B // 2)
            ref[to : to + B // 2, at] = jnp.where(own, cov_ref[rows, k * B : N], zero)
    rows_low_ref[...] = jnp.where(col == 0, cov_ref[: N // 2, :N], zero)
    rows_high_ref[...] = jnp.where(col == 0, cov_ref[N // 2 :, :N], zero)


def prepare(place, cov):
    vm = pl.BlockSpec(memory_space=pltpu.VMEM)
    folded = pltpu.VMEM((FOLD_ROWS // 2, FOLD), cov.dtype)
    rows = pltpu.HBM((N // 2, N), cov.dtype)
    return pl.pallas_call(
        prepare_kernel,
        out_shape=[folded, folded, rows, rows],
        in_specs=[pl.BlockSpec(memory_space=pltpu.SMEM), vm],
        out_specs=[vm, vm, vm, vm],
        compiler_params=pltpu.CompilerParams(vmem_limit_bytes=16 << 20),
        name="prepare",
    )(place, cov)


def eliminate(k, s_ref, w_ref, base):
    lo, hi = k * B, (k + 1) * B
    inv = invert_factor(s_ref[lo - base : hi - base, lo - base : hi - base])
    w_ref[lo:hi, lo:hi] = inv
    if k:
        w_ref[lo:hi, :lo] = mm(inv, w_ref[lo:hi, :lo])
    if hi < N:
        u = mm(inv, s_ref[lo - base : hi - base, hi - base :])
        for q in range(k + 1, STEPS):
            a, b = q * B, (q + 1) * B
            uq = u[:, a - hi : b - hi]
            at = slice(a - base, b - base)
            s_ref[at, a - base :] = s_ref[at, a - base :] - mm_t(uq, u[:, a - hi :])
            w_ref[a:b, :hi] = w_ref[a:b, :hi] - mm_t(uq, w_ref[lo:hi, :hi])


def write_out(pairs, sem):
    copies = [pltpu.make_async_copy(src, dst, sem.at[i]) for i, (src, dst) in enumerate(pairs)]
    for copy in copies:
        copy.start()
    for copy in copies:
        copy.wait()


def factor_kernel(a_ref, hi_out, lo_out, s_ref, w_ref, hi_ref, lo_ref, sem):
    for k in range(BANDS):
        band = a_ref[k * B : (k + 1) * B, :].astype(jnp.float32)
        j = STEPS - 1 - k
        s_ref[k * B : (k + 1) * B, k * B :] = band[:, : N - k * B]
        s_ref[j * B : (j + 1) * B, j * B :] = band[:, N - k * B :]
    w_ref[...] = jnp.zeros_like(w_ref)
    for k in range(STEPS):
        eliminate(k, s_ref, w_ref, 0)
    w = w_ref[...]
    high = w.astype(jnp.bfloat16)
    hi_ref[...] = high
    lo_ref[...] = (w - high.astype(jnp.float32)).astype(jnp.bfloat16)
    write_out([(hi_ref, hi_out), (lo_ref, lo_out)], sem)


def factor(folded):
    vm = pl.BlockSpec(memory_space=pltpu.VMEM)
    hbm = pl.BlockSpec(memory_space=pltpu.HBM)
    f32, low = pltpu.VMEM((N, N), jnp.float32), pltpu.VMEM((N, N), jnp.bfloat16)
    return pl.pallas_call(
        factor_kernel,
        out_shape=[pltpu.HBM((N, N), jnp.bfloat16)] * 2,
        in_specs=[vm],
        out_specs=[hbm, hbm],
        scratch_shapes=[f32, f32, low, low, pltpu.SemaphoreType.DMA((2,))],
        compiler_params=pltpu.CompilerParams(vmem_limit_bytes=16 << 20),
        cost_estimate=pl.CostEstimate(flops=40_000_000_000, bytes_accessed=4_000_000, transcendentals=0),
        name="factor",
    )(folded)


TILE = 256
PANEL = 256


def update_kernel(where_ref, cov_ref, rows_ref, cols_ref, hi_ref, lo_ref, out_ref, left_ref):
    row, col = where_ref[0], where_ref[1]
    step = pl.program_id(0)

    @pl.when(step == 0)
    def _():
        for k in range(N // PANEL):
            lo, hi = k * PANEL, (k + 1) * PANEL
            part = jnp.zeros((rows_ref.shape[0], PANEL), jnp.float32)
            for w_ref in (hi_ref, lo_ref):
                part += lax.dot_general(
                    rows_ref[:, :hi],
                    w_ref[lo:hi, :hi],
                    (((1,), (1,)), ((), ())),
                    preferred_element_type=jnp.float32,
                )
            left_ref[:, lo:hi] = part.astype(jnp.bfloat16)

    half = lax.div(step, N // TILE)
    panel = cols_ref[...]
    parts = []
    for k in range(N // PANEL):
        lo, hi = k * PANEL, (k + 1) * PANEL
        part = jnp.dot(hi_ref[lo:hi, :hi], panel[:hi], preferred_element_type=jnp.float32)
        part += jnp.dot(lo_ref[lo:hi, :hi], panel[:hi], preferred_element_type=jnp.float32)
        parts.append(part.astype(jnp.bfloat16))
    right = jnp.concatenate(parts, axis=0)
    product = jnp.dot(left_ref[...], right, preferred_element_type=jnp.float32)
    value = (cov_ref[...].astype(jnp.float32) - product).astype(jnp.bfloat16)
    keep = jnp.logical_and(row > 0, jnp.logical_or(col > 0, half > 0))
    out_ref[...] = jnp.where(keep, value, jnp.zeros_like(value))


def update(place, cov, rows, cols, hi, lo):
    n_rows, n_cols = cov.shape
    vm = pl.BlockSpec(memory_space=pltpu.VMEM)
    tile = pl.BlockSpec((n_rows, TILE), lambda j: (0, j))
    return pl.pallas_call(
        update_kernel,
        out_shape=jax.ShapeDtypeStruct(cov.shape, jnp.bfloat16),
        grid=(n_cols // TILE,),
        in_specs=[pl.BlockSpec(memory_space=pltpu.SMEM), tile, vm, pl.BlockSpec((N, TILE), lambda j: (0, j)), vm, vm],
        out_specs=tile,
        scratch_shapes=[pltpu.VMEM((n_rows, N), jnp.bfloat16)],
        compiler_params=pltpu.CompilerParams(vmem_limit_bytes=24 << 20),
        name="update",
    )(place, cov, rows, cols, hi, lo)


DEPTH = 8
PART = N // 4
AXES = ("row", "col")


def device(x, y, z, core):
    return ((x % 4 * 4 + y % 4) * 2 + core) * 2 * DEPTH + (y % 8 // 4) * DEPTH + z % DEPTH


def send(x, pairs):
    return lax.ppermute(x, AXES, pairs)


def chips(xs, ys, zs):
    return [(x, y, z) for x in xs for y in ys for z in zs]


def shifts(sources, by, cores=(0,)):
    return [
        (device(x, y, z, c), device(x + by[0], y + by[1], z + by[2], c)) for x, y, z in sources for c in cores
    ]


def halve(low, high, sources, by, cores=(0,)):
    return low + send(high, shifts(sources, by, cores))


def scatter(x, size, sources, offsets):
    sent = [send(x[i * size : (i + 1) * size], shifts(sources, by)) for i, by in enumerate(offsets, 1)]
    return sum(sent, x[:size])


def halves(x):
    return x[: x.shape[0] // 2], x[x.shape[0] // 2 :]


def double(x, sources, by, cores=(0,)):
    return x + send(x, shifts(sources, by, cores))


def gather(x, axis, groups):
    copies = jnp.broadcast_to(x[None], (4, *x.shape)).reshape(4 * x.shape[0], x.shape[1])
    return lax.all_to_all(copies, axis, 0, 0, axis_index_groups=groups, tiled=True)


SAME_X = [[8 * x + i for x in range(4)] for i in range(8)]
SAME_Z = [[8 * y + odd + 2 * z for z in range(4)] for y in range(2) for odd in range(2)]


def in_hbm(x):
    return pltpu.with_memory_space_constraint(x, pltpu.HBM)


def per_device(covariance):
    row = lax.axis_index("row")
    col = lax.axis_index("col")
    place = jnp.stack([row, col]).astype(jnp.int32)
    both = (0, 1)
    all_x, even_z, all_z = range(4), range(0, 8, 2), range(8)
    low, high, rows_low, rows_high = prepare(place, covariance)

    together = lambda *arrays: lax.optimization_barrier(arrays)
    lead = halve(low, high, [(0, 0, 0)], (2, 0, 0))
    rows = halve(rows_low, rows_high, chips(all_x, range(4), [0]), (0, 0, 4), both)
    lead = halve(*halves(lead), chips([0, 2], [0], [0]), (1, 0, 0))
    lead, covariance_late = together(lead, covariance)
    cols = jnp.where(row == 0, covariance_late, 0)
    cols = scatter(cols, N // 4, chips([0], [0, 4], all_z), [(1, 0, 0), (2, 0, 0), (3, 0, 0)])
    lead = double(lead, chips(all_x, [0], [0]), (0, 4, 0))
    lead = double(lead, chips(all_x, [0, 4], [0]), (0, 2, 0))
    lead, rows = together(lead, rows)
    rows = halve(*halves(rows), chips(all_x, range(4), [0, 4]), (0, 0, 2), both)
    lead = double(lead, chips(all_x, even_z, [0]), (0, 1, 0))
    lead, cols = together(lead, cols)
    cols = scatter(cols, N // 16, chips(all_x, [0, 4], all_z), [(0, 1, 0), (0, 2, 0), (0, 3, 0)])
    lead = double(lead, chips(all_x, all_z, [0]), (0, 0, 4))
    lead, rows, cols = together(lead, rows, cols)
    rows = double(rows, chips(all_x, range(4), even_z), (0, 0, 1), both)
    kept, passed = halves(cols)
    pairs = [(2 * chip, 2 * chip + 1) for chip in range(16)]
    cols = jnp.where(row % 2 == 0, kept, lax.ppermute(passed, "row", pairs))
    lead = double(lead, chips(all_x, all_z, [0, 4]), (0, 0, 2))
    lead, rows, cols = together(lead, rows, cols)
    rows = double(rows, chips(all_x, range(4), all_z), (0, 4, 0), both)
    cols = lax.all_gather(cols, "row", axis=0, tiled=True)
    lead = double(lead, chips(all_x, all_z, even_z), (0, 0, 1))
    lead = lead + lax.ppermute(lead, "row", pairs)
    lead, rows = together(lead, rows)
    lead = gather(lead, "row", SAME_X)
    rows = gather(rows, "col", SAME_Z)
    hi, lo = factor(in_hbm(lead))
    return update(place, in_hbm(covariance), rows, in_hbm(cols), in_hbm(hi), in_hbm(lo))


def solution(mesh):
    return jax.shard_map(
        per_device,
        mesh=mesh,
        in_specs=(P("row", "col"),),
        out_specs=P("row", "col"),
        check_vma=False,
    )
```

```python
import jax
import jax.numpy as jnp
from jax import lax
from jax.experimental import pallas as pl
from jax.experimental.pallas import tpu as pltpu
from jax.sharding import PartitionSpec as P

N = 768
B = 128
STEPS = N // B


def split(x):
    high = x.astype(jnp.bfloat16)
    return high, (x - high.astype(jnp.float32)).astype(jnp.bfloat16)


def product(a, b, dim):
    dot = lambda x, y: lax.dot_general(x, y, (((dim,), (0,)), ((), ())), preferred_element_type=jnp.float32)
    (a_high, a_low), (b_high, b_low) = split(a), split(b)
    return dot(a_high, b_high) + (dot(a_high, b_low) + dot(a_low, b_high))


def mm(a, b):
    return product(a, b, 1)


def mm_t(a, b):
    return product(a, b, 0)


def invert_factor(block):
    groups = B // 8
    lane = lax.broadcasted_iota(jnp.int32, (8, B), 1)
    sub = lax.broadcasted_iota(jnp.int32, (8, B), 0)
    left = [block[8 * g : 8 * g + 8] for g in range(groups)]
    right = [jnp.where(lane == sub + 8 * g, 1.0, 0.0).astype(jnp.float32) for g in range(groups)]
    done = []

    def over_rows(x, i):
        return jnp.broadcast_to(x[i : i + 1], (8, B))

    def over_lanes(x, i):
        return jnp.broadcast_to(x[:, i : i + 1], (8, B))

    for g in range(groups):
        first = 8 * g
        last = g == groups - 1
        row_l, row_r = left[g], right[g]
        own = [over_lanes(row_l, first + i) for i in range(8)]
        if not last:
            nxt_l, nxt_r = left[g + 1], right[g + 1]
            nxt = [over_lanes(nxt_l, first + i) for i in range(8)]
        pivot = jnp.ones((8, B), jnp.float32)
        for i in range(8):
            d = over_rows(own[i], i)
            r = 1.0 / d
            pivot = jnp.where(sub == i, d, pivot)
            m = jnp.where(sub > i, own[i] * r, 0.0)
            rows = [over_rows(own[t], i) for t in range(i + 1, 8)]
            for t in range(i + 1, 8):
                own[t] = own[t] - m * rows[t - i - 1]
            rl, rr = over_rows(row_l, i), over_rows(row_r, i)
            row_l = row_l - m * rl
            row_r = row_r - m * rr
            if not last:
                n = nxt[i] * r
                for t in range(i + 1, 8):
                    nxt[t] = nxt[t] - n * rows[t - i - 1]
                nxt_l = nxt_l - n * rl
                nxt_r = nxt_r - n * rr
        scale = lax.rsqrt(pivot)
        done.append(row_r * scale)
        if not last:
            left[g + 1], right[g + 1] = nxt_l, nxt_r
        if g + 2 < groups:
            ul = row_l * scale
            cut = jnp.where(lane >= first + 16, ul, 0.0)
            both = mm_t(cut, jnp.concatenate([ul, row_r * scale], axis=1))
            for q in range(g + 2, groups):
                left[q] = left[q] - both[8 * q : 8 * q + 8, :B]
                right[q] = right[q] - both[8 * q : 8 * q + 8, B:]
    return jnp.concatenate(done, axis=0)


BANDS = STEPS // 2
FOLD = (STEPS + 1) * B
FOLD_ROWS = BANDS * B


def prepare_kernel(where_ref, cov_ref, low_ref, high_ref, rows_low_ref, rows_high_ref):
    row, col = where_ref[0], where_ref[1]
    own = jnp.logical_and(row == 0, col == 0)
    zero = jnp.zeros((), cov_ref.dtype)
    half = FOLD_ROWS // 2
    for k in range(STEPS):
        j = min(k, STEPS - 1 - k)
        at = slice(0, N - k * B) if j == k else slice(N - j * B, FOLD)
        for first in range(0, B, B // 2):
            to = j * B + first
            ref, to = (low_ref, to) if to < half else (high_ref, to - half)
            rows = slice(k * B + first, k * B + first + B // 2)
            ref[to : to + B // 2, at] = jnp.where(own, cov_ref[rows, k * B : N], zero)
    rows_low_ref[...] = jnp.where(col == 0, cov_ref[: N // 2, :N], zero)
    rows_high_ref[...] = jnp.where(col == 0, cov_ref[N // 2 :, :N], zero)


def prepare(place, cov):
    vm = pl.BlockSpec(memory_space=pltpu.VMEM)
    folded = pltpu.VMEM((FOLD_ROWS // 2, FOLD), cov.dtype)
    rows = pltpu.HBM((N // 2, N), cov.dtype)
    return pl.pallas_call(
        prepare_kernel,
        out_shape=[folded, folded, rows, rows],
        in_specs=[pl.BlockSpec(memory_space=pltpu.SMEM), vm],
        out_specs=[vm, vm, vm, vm],
        compiler_params=pltpu.CompilerParams(vmem_limit_bytes=16 << 20),
        name="prepare",
    )(place, cov)


def eliminate(k, s_ref, w_ref, base):
    lo, hi = k * B, (k + 1) * B
    inv = invert_factor(s_ref[lo - base : hi - base, lo - base : hi - base])
    w_ref[lo:hi, lo:hi] = inv
    if k:
        w_ref[lo:hi, :lo] = mm(inv, w_ref[lo:hi, :lo])
    if hi < N:
        u = mm(inv, s_ref[lo - base : hi - base, hi - base :])
        for q in range(k + 1, STEPS):
            a, b = q * B, (q + 1) * B
            uq = u[:, a - hi : b - hi]
            at = slice(a - base, b - base)
            s_ref[at, a - base :] = s_ref[at, a - base :] - mm_t(uq, u[:, a - hi :])
            w_ref[a:b, :hi] = w_ref[a:b, :hi] - mm_t(uq, w_ref[lo:hi, :hi])


def write_out(pairs, sem):
    copies = [pltpu.make_async_copy(src, dst, sem.at[i]) for i, (src, dst) in enumerate(pairs)]
    for copy in copies:
        copy.start()
    for copy in copies:
        copy.wait()


def factor_kernel(a_ref, hi_out, lo_out, s_ref, w_ref, hi_ref, lo_ref, sem):
    for k in range(BANDS):
        band = a_ref[k * B : (k + 1) * B, :].astype(jnp.float32)
        j = STEPS - 1 - k
        s_ref[k * B : (k + 1) * B, k * B :] = band[:, : N - k * B]
        s_ref[j * B : (j + 1) * B, j * B :] = band[:, N - k * B :]
    w_ref[...] = jnp.zeros_like(w_ref)
    for k in range(STEPS):
        eliminate(k, s_ref, w_ref, 0)
    w = w_ref[...]
    high = w.astype(jnp.bfloat16)
    hi_ref[...] = high
    lo_ref[...] = (w - high.astype(jnp.float32)).astype(jnp.bfloat16)
    write_out([(hi_ref, hi_out), (lo_ref, lo_out)], sem)


def factor(folded):
    vm = pl.BlockSpec(memory_space=pltpu.VMEM)
    hbm = pl.BlockSpec(memory_space=pltpu.HBM)
    f32, low = pltpu.VMEM((N, N), jnp.float32), pltpu.VMEM((N, N), jnp.bfloat16)
    return pl.pallas_call(
        factor_kernel,
        out_shape=[pltpu.HBM((N, N), jnp.bfloat16)] * 2,
        in_specs=[vm],
        out_specs=[hbm, hbm],
        scratch_shapes=[f32, f32, low, low, pltpu.SemaphoreType.DMA((2,))],
        compiler_params=pltpu.CompilerParams(vmem_limit_bytes=16 << 20),
        cost_estimate=pl.CostEstimate(flops=40_000_000_000, bytes_accessed=4_000_000, transcendentals=0),
        name="factor",
    )(folded)


TILE = 256
PANEL = 256


def update_kernel(where_ref, cov_ref, rows_ref, cols_ref, hi_ref, lo_ref, out_ref, left_ref):
    row, col = where_ref[0], where_ref[1]
    step = pl.program_id(0)

    @pl.when(step == 0)
    def _():
        for k in range(N // PANEL):
            lo, hi = k * PANEL, (k + 1) * PANEL
            part = jnp.zeros((rows_ref.shape[0], PANEL), jnp.float32)
            for w_ref in (hi_ref, lo_ref):
                part += lax.dot_general(
                    rows_ref[:, :hi],
                    w_ref[lo:hi, :hi],
                    (((1,), (1,)), ((), ())),
                    preferred_element_type=jnp.float32,
                )
            left_ref[:, lo:hi] = part.astype(jnp.bfloat16)

    half = lax.div(step, N // TILE)
    panel = cols_ref[...]
    parts = []
    for k in range(N // PANEL):
        lo, hi = k * PANEL, (k + 1) * PANEL
        part = jnp.dot(hi_ref[lo:hi, :hi], panel[:hi], preferred_element_type=jnp.float32)
        part += jnp.dot(lo_ref[lo:hi, :hi], panel[:hi], preferred_element_type=jnp.float32)
        parts.append(part.astype(jnp.bfloat16))
    right = jnp.concatenate(parts, axis=0)
    product = jnp.dot(left_ref[...], right, preferred_element_type=jnp.float32)
    value = (cov_ref[...].astype(jnp.float32) - product).astype(jnp.bfloat16)
    keep = jnp.logical_and(row > 0, jnp.logical_or(col > 0, half > 0))
    out_ref[...] = jnp.where(keep, value, jnp.zeros_like(value))


def update(place, cov, rows, cols, hi, lo):
    n_rows, n_cols = cov.shape
    vm = pl.BlockSpec(memory_space=pltpu.VMEM)
    tile = pl.BlockSpec((n_rows, TILE), lambda j: (0, j))
    return pl.pallas_call(
        update_kernel,
        out_shape=jax.ShapeDtypeStruct(cov.shape, jnp.bfloat16),
        grid=(n_cols // TILE,),
        in_specs=[pl.BlockSpec(memory_space=pltpu.SMEM), tile, vm, pl.BlockSpec((N, TILE), lambda j: (0, j)), vm, vm],
        out_specs=tile,
        scratch_shapes=[pltpu.VMEM((n_rows, N), jnp.bfloat16)],
        compiler_params=pltpu.CompilerParams(vmem_limit_bytes=24 << 20),
        name="update",
    )(place, cov, rows, cols, hi, lo)


DEPTH = 8
PART = N // 4
AXES = ("row", "col")


def device(x, y, z, core):
    return ((x % 4 * 4 + y % 4) * 2 + core) * 2 * DEPTH + (y % 8 // 4) * DEPTH + z % DEPTH


def send(x, pairs):
    return lax.ppermute(x, AXES, pairs)


def chips(xs, ys, zs):
    return [(x, y, z) for x in xs for y in ys for z in zs]


def shifts(sources, by, cores=(0,)):
    return [
        (device(x, y, z, c), device(x + by[0], y + by[1], z + by[2], c)) for x, y, z in sources for c in cores
    ]


def halve(low, high, sources, by, cores=(0,)):
    return low + send(high, shifts(sources, by, cores))


def scatter(x, size, sources, offsets):
    sent = [send(x[i * size : (i + 1) * size], shifts(sources, by)) for i, by in enumerate(offsets, 1)]
    return sum(sent, x[:size])


def halves(x):
    return x[: x.shape[0] // 2], x[x.shape[0] // 2 :]


def double(x, sources, by, cores=(0,)):
    return x + send(x, shifts(sources, by, cores))


def gather(x, axis, groups):
    copies = jnp.broadcast_to(x[None], (4, *x.shape)).reshape(4 * x.shape[0], x.shape[1])
    return lax.all_to_all(copies, axis, 0, 0, axis_index_groups=groups, tiled=True)


SAME_X = [[8 * x + i for x in range(4)] for i in range(8)]
SAME_Z = [[8 * y + odd + 2 * z for z in range(4)] for y in range(2) for odd in range(2)]


def in_hbm(x):
    return pltpu.with_memory_space_constraint(x, pltpu.HBM)


def per_device(covariance):
    row = lax.axis_index("row")
    col = lax.axis_index("col")
    place = jnp.stack([row, col]).astype(jnp.int32)
    both = (0, 1)
    all_x, even_z, all_z = range(4), range(0, 8, 2), range(8)
    low, high, rows_low, rows_high = prepare(place, covariance)

    together = lambda *arrays: lax.optimization_barrier(arrays)
    lead = halve(low, high, [(0, 0, 0)], (2, 0, 0))
    rows = halve(rows_low, rows_high, chips(all_x, range(4), [0]), (0, 0, 4), both)
    lead = halve(*halves(lead), chips([0, 2], [0], [0]), (1, 0, 0))
    lead, covariance_late = together(lead, covariance)
    cols = jnp.where(row == 0, covariance_late, 0)
    cols = scatter(cols, N // 4, chips([0], [0, 4], all_z), [(1, 0, 0), (2, 0, 0), (3, 0, 0)])
    lead = double(lead, chips(all_x, [0], [0]), (0, 4, 0))
    lead = double(lead, chips(all_x, [0, 4], [0]), (0, 2, 0))
    lead, rows = together(lead, rows)
    rows = halve(*halves(rows), chips(all_x, range(4), [0, 4]), (0, 0, 2), both)
    lead = double(lead, chips(all_x, even_z, [0]), (0, 1, 0))
    lead, cols = together(lead, cols)
    cols = scatter(cols, N // 16, chips(all_x, [0, 4], all_z), [(0, 1, 0), (0, 2, 0), (0, 3, 0)])
    lead = double(lead, chips(all_x, all_z, [0]), (0, 0, 4))
    lead, rows, cols = together(lead, rows, cols)
    rows = double(rows, chips(all_x, range(4), even_z), (0, 0, 1), both)
    kept, passed = halves(cols)
    pairs = [(2 * chip, 2 * chip + 1) for chip in range(16)]
    cols = jnp.where(row % 2 == 0, kept, lax.ppermute(passed, "row", pairs))
    lead = double(lead, chips(all_x, all_z, [0, 4]), (0, 0, 2))
    lead, rows, cols = together(lead, rows, cols)
    rows = double(rows, chips(all_x, range(4), all_z), (0, 4, 0), both)
    cols = lax.all_gather(cols, "row", axis=0, tiled=True)
    lead = double(lead, chips(all_x, all_z, even_z), (0, 0, 1))
    lead = lead + lax.ppermute(lead, "row", pairs)
    lead = gather(lead, "row", SAME_X)
    rows = gather(rows, "col", SAME_Z)
    hi, lo = factor(in_hbm(lead))
    return update(place, in_hbm(covariance), rows, in_hbm(cols), in_hbm(hi), in_hbm(lo))


def solution(mesh):
    return jax.shard_map(
        per_device,
        mesh=mesh,
        in_specs=(P("row", "col"),),
        out_specs=P("row", "col"),
        check_vma=False,
    )
```
